256 devices in a mesh: tm: 32 (over x, z), inp: 4 (over y), integ: 2 (over core).
Axes of the slice: x: 4, y: 4, z: 8, core: 2. Of those that a mesh axis runs over, the one named last changes fastest.
Arguments:
- voltages: bfloat16 [256, 2, 256, 1024], P(('tm', 'integ'), None, None, 'inp'), may hold values from -6 to 6
- taps_coef: float32 [16, 256], replicated, may hold values from -1.5 to 1.5
- station_map: int32 [1024], replicated, may hold values from 0 to 1023, each once
- flags: int32 [1024], P('inp'), may hold values 0 or 1
Outputs:
- visibilities: float32 [256, 2, 1024, 1024], P(('tm', 'integ'), None, 'inp')
The draws below stay inside these ranges and needn't reach their ends.
Inputs may be any that keep to these rules, and one draw needn't show every extreme that they name: station_map names every input once.
All inputs are finite; a program needn't handle non-finite values. No bound on the sum of `flags` on one device may be relied on, other than what follows from the above.
Results may differ from the reference program's by a relative error of at most 0.0036.
Values may be sent and summed in bfloat16 or wider, within the bound.
No kernel may reach another device: no remote copies, remote signals or barrier semaphores. Data moves between devices by JAX's collectives and lax.ppermute only.
A program may use at most 64 MiB of HBM per device.

```python
import math
import jax
import jax.numpy as jnp
from jax import lax

S = 1024
CH = 256
TAPS = 16
FRAMES = 256


def set_ends(array, rng, smallest, high):
    spot = [jax.random.randint(jax.random.fold_in(rng, axis), (), 0, length) for axis, length in enumerate(array.shape)]
    main_axis = array.shape.index(max(array.shape))
    next_to = spot[:main_axis] + [(spot[main_axis] + 1) % array.shape[main_axis]] + spot[main_axis + 1:]
    return array.at[tuple(spot)].set(smallest).at[tuple(next_to)].set(high)


def level_of(stream_key, shape, shards, smallest, largest):
    factor_of, own = 1.0, jax.random.fold_in(stream_key, 6)
    for axis_at, blocks in shards:
        draws = jnp.exp(jax.random.uniform(jax.random.fold_in(own, axis_at), (blocks,), jnp.float32, smallest / len(shards), largest / len(shards)))
        factor_of = factor_of * jnp.repeat(draws, shape[axis_at] // blocks).reshape([-1 if axis == axis_at else 1 for axis in range(len(shape))])
    return factor_of


def centred(stream_key, shape, deviation, most, shards=(), kind=jnp.bfloat16):
    array = deviation * jax.random.normal(stream_key, shape, jnp.float32)
    if shards:
        array = array * level_of(stream_key, shape, shards, -0.22, 0.18)
    return jnp.clip(array, -most, most).astype(kind)


def setup_inputs(seed: int = 0) -> dict:
    streams_of = jax.random.split(jax.random.key(seed), 5)
    return {
        "voltages": centred(streams_of[0], (FRAMES, 2, CH, S), 1.0, 6.0, ((0, 64), (3, 4))),
        "taps_coef": centred(streams_of[1], (TAPS, CH), TAPS ** -0.5, 1.5, (), jnp.float32),
        "station_map": jax.random.permutation(streams_of[2], S).astype(jnp.int32),
        "flags": set_ends((jax.random.randint(streams_of[3], (S,), 0, 8) < 1).astype(jnp.int32), jax.random.fold_in(streams_of[3], 1), 0, 1),
    }


def fourier_table(channels):
    grid = jnp.arange(channels, dtype=jnp.int32)
    phase_index = grid[:, None] * grid[None, :] % channels
    angles = phase_index.astype(jnp.float32) * (2.0 * math.pi / channels)
    output_scale = 1.0 / math.sqrt(channels)
    cosine = jnp.cos(angles) * output_scale
    sine = jnp.sin(angles) * output_scale
    return jnp.stack([jnp.stack([cosine, sine]), jnp.stack([-sine, cosine])])

def channelize(block_volt, taps_coef, block_flag_values):
    total_frames = block_volt.shape[0]
    zero_padding = jnp.zeros((TAPS - 1,) + block_volt.shape[1:], jnp.bfloat16)
    extended = jnp.concatenate([zero_padding, block_volt], axis=0)
    windowed = jnp.zeros(block_volt.shape, jnp.float32)
    for tap_index in range(TAPS):
        windowed = windowed + taps_coef[tap_index][None, None, :, None] * extended[tap_index:tap_index + total_frames].astype(jnp.float32)
    dft_table = fourier_table(CH)
    channel_spectra = jnp.einsum('oicn,fina->foca', dft_table, windowed, precision=lax.Precision.HIGHEST)
    valid_blocks = (1 - block_flag_values).astype(jnp.float32)
    return (channel_spectra * valid_blocks[None, None, None, :]).astype(jnp.bfloat16)

def reference(voltages, taps_coef, station_map, flags):
    block_width = min(S, 128)
    block_count = S // block_width
    blocks = voltages.reshape(FRAMES, 2, CH, block_count, block_width).transpose(3, 0, 1, 2, 4)
    flag_blocks = flags.reshape(block_count, block_width)
    channel_spectra = lax.map(lambda pair: channelize(pair[0], taps_coef, pair[1]), (blocks, flag_blocks))
    channel_spectra = channel_spectra.transpose(3, 1, 2, 0, 4).reshape(CH, FRAMES, 2, S)

    def per_channel(channel_spec):
        ordered = channel_spec[:, :, station_map]
        reversed_order = jnp.stack([ordered[:, 1], -ordered[:, 0]], axis=1)
        ordered_rows = ordered.reshape(FRAMES * 2, S)
        flipped_rows = reversed_order.reshape(FRAMES * 2, S)
        real_part = jnp.dot(ordered_rows.T, ordered_rows, preferred_element_type=jnp.float32)
        imag_part = jnp.dot(flipped_rows.T, ordered_rows, preferred_element_type=jnp.float32)
        return jnp.stack([real_part, imag_part]) * (1.0 / FRAMES)
    return lax.map(per_channel, channel_spectra)
```

```python
import functools
import math

import jax
import jax.numpy as jnp
import ml_dtypes
import numpy as np
from jax import lax
from jax.experimental import pallas as pl
from jax.experimental.pallas import tpu as pltpu
from jax.sharding import PartitionSpec as P

TIME = ("tm", "integ")
BF16, F32 = jnp.bfloat16, jnp.float32
LANES = 128


def fourier_table(channels):
    grid = np.arange(channels)
    angles = (grid[:, None] * grid[None, :] % channels) * (2.0 * math.pi / channels)
    cosine = np.cos(angles) / math.sqrt(channels)
    sine = np.sin(angles) / math.sqrt(channels)
    table = np.block([[cosine, sine], [-sine, cosine]])
    high = table.astype(ml_dtypes.bfloat16)
    low = (table - high.astype(np.float64)).astype(ml_dtypes.bfloat16)
    return jnp.asarray(high), jnp.asarray(low)


def filter_kernel(
    taps, frames, parts, place, same, cross, left_same, left_cross, right_same, right_cross,
    coef, high, low, valid, *rest
):
    outs, (held, w_high, w_low, turned) = rest[:parts], rest[parts:]
    core, wraps = place[0], place[1]
    half = frames // 2
    samples = same.shape[2]
    first = core * half
    second = (1 - core) * half
    for start, mine, theirs in (
        (0, left_same, left_cross),
        (frames, same, cross),
        (2 * frames, right_same, right_cross),
    ):
        held[pl.ds(start + first, half)] = mine[...]
        held[pl.ds(start + second, half)] = theirs[...]

    @pl.when(wraps == 1)
    def _():
        held[frames : 2 * frames] = jnp.zeros((frames,) + same.shape[1:], BF16)

    rows = 16

    def one_block(block, carry):
        at = pl.multiple_of(block * rows, rows)
        factors = [coef[p, pl.ds(at, rows), :] for p in range(taps)]
        for part in range(2):
            sums = [None] * frames
            for j in range(2 * frames - taps + 1, 3 * frames):
                x = held[j, part, pl.ds(at, rows), :].astype(F32)
                for o in range(frames):
                    p = j - (2 * frames - taps + 1) - o
                    if 0 <= p < taps:
                        term = factors[p] * x
                        sums[o] = term if sums[o] is None else sums[o] + term
            for o in range(frames):
                top = sums[o].astype(BF16)
                rest_of = (sums[o] - top.astype(F32)).astype(BF16)
                lanes = slice((o % 2) * LANES, (o % 2 + 1) * LANES)
                to = pl.ds(pl.multiple_of(part * samples + at, rows), rows)
                w_high[o // 2, to, lanes] = top
                w_low[o // 2, to, lanes] = rest_of
        return carry

    lax.fori_loop(0, samples // rows, one_block, 0)

    keep = valid[...]
    channels = samples
    for pair in range(frames // 2):
        block = jnp.dot(high[...], w_high[pair], preferred_element_type=F32)
        block += jnp.dot(high[...], w_low[pair], preferred_element_type=F32)
        block += jnp.dot(low[...], w_high[pair], preferred_element_type=F32)
        for which in range(2):
            o = pair * 2 + which
            for part in range(2):
                piece = block[part * channels : (part + 1) * channels, which * LANES : (which + 1) * LANES]
                turned[pl.ds(part * frames + o, channels, stride=2 * frames), :] = piece * keep

    depth = 2 * frames
    dests, per_part = outs[0].shape[0], outs[0].shape[1]

    def one_dest(dest, carry):
        for n, out in enumerate(outs):
            at = pl.multiple_of((dest * parts + n) * per_part, per_part)
            out[dest] = turned[pl.ds(at, per_part), :].astype(BF16)
        return carry

    lax.fori_loop(0, dests, one_dest, 0)


def filter_bank(place, blocks, coef, high, low, valid, dests, parts):
    taps, samples, _ = coef.shape
    frames = 2 * blocks[0].shape[0]
    per_part = samples // dests // parts * 2 * frames
    vmem = pl.BlockSpec(memory_space=pltpu.VMEM)
    return pl.pallas_call(
        functools.partial(filter_kernel, taps, frames, parts),
        out_shape=[jax.ShapeDtypeStruct((dests, per_part, LANES), BF16)] * parts,
        in_specs=[pl.BlockSpec(memory_space=pltpu.SMEM)] + [vmem] * 10,
        out_specs=[vmem] * parts,
        scratch_shapes=[
            pltpu.VMEM((3 * frames, 2, samples, LANES), BF16),
            pltpu.VMEM((frames // 2, 2 * samples, 2 * LANES), BF16),
            pltpu.VMEM((frames // 2, 2 * samples, 2 * LANES), BF16),
            pltpu.VMEM((samples * 2 * frames, LANES), F32),
        ],
        compiler_params=pltpu.CompilerParams(vmem_limit_bytes=48 * 2**20),
        name="filter_bank",
    )(place, *blocks, coef, high, low, valid)


def correlate_kernel(scale, cores, part_rows, row_at, *refs):
    blocks, (pick, pick_rows, *_), out = refs[:4], refs[4:-1], refs[-1]
    channel = pl.program_id(0)
    at = pl.multiple_of(channel * part_rows, part_rows)
    columns = []
    for block in blocks:
        for core in range(cores):
            tile = block[:, core, pl.ds(at, part_rows), :]
            columns.append(tile.reshape(-1, LANES))
    gathered = jnp.concatenate(columns, axis=1)
    lhs = lax.dot_general(
        pick_rows[...], gathered, (((1,), (1,)), ((), ())), preferred_element_type=F32
    ).astype(BF16)
    ordered = jnp.dot(gathered, pick[...], preferred_element_type=F32)
    half = part_rows // 2
    split = ordered.reshape(-1, 2, half, ordered.shape[1])
    direct = ordered.astype(BF16)
    flipped = jnp.stack([-split[:, 1], split[:, 0]], axis=1).reshape(ordered.shape).astype(BF16)
    out[0, 0] = jnp.dot(lhs, direct, preferred_element_type=F32) * scale
    out[0, 1] = jnp.dot(lhs, flipped, preferred_element_type=F32) * scale


def correlate(blocks, pick, pick_rows, scale, part_rows, shape, first, so_far):
    count = blocks[0].shape[2] // part_rows
    whole = lambda a: pl.BlockSpec(a.shape, lambda i: (0,) * a.ndim)
    operands = [*blocks, pick, pick_rows]
    specs = [whole(a) for a in operands]
    aliases = {}
    if so_far is not None:
        operands.append(so_far)
        specs.append(pl.BlockSpec(memory_space=pl.ANY))
        aliases = {len(operands) - 1: 0}
    body = functools.partial(correlate_kernel, scale, blocks[0].shape[1], part_rows, None)
    return pl.pallas_call(
        body,
        grid=(count,),
        out_shape=jax.ShapeDtypeStruct(shape, F32),
        in_specs=specs,
        out_specs=pl.BlockSpec((1,) + shape[1:], lambda i: (first + i, 0, 0, 0)),
        input_output_aliases=aliases,
        compiler_params=pltpu.CompilerParams(vmem_limit_bytes=48 * 2**20),
        name="correlate",
    )(*operands)


def local(voltages, taps_coef, station_map, flags):
    frames, _, samples, width = voltages.shape
    chips, cores, rows = lax.axis_size("tm"), lax.axis_size("integ"), lax.axis_size("inp")
    chip, core, row = lax.axis_index("tm"), lax.axis_index("integ"), lax.axis_index("inp")
    index = lambda t, c: t * cores + c
    same = lax.dynamic_slice_in_dim(voltages, core * LANES, LANES, axis=3)
    cross = lax.dynamic_slice_in_dim(voltages, (1 - core) * LANES, LANES, axis=3)

    def route(step, swap):
        pairs = []
        for t in range(chips):
            source = t - step
            if step == 1 and t in (0, chips - 1):
                continue
            for c in range(cores):
                pairs.append((index(source % chips, c ^ swap), index(t, c)))
        return pairs

    with jax.named_scope("halo"):
        right_cross = lax.ppermute(cross, TIME, route(-1, 1))
        left_cross = lax.ppermute(cross, TIME, route(1, 1))
        right_same = lax.ppermute(same, TIME, route(-1, 0))
        left_same = lax.ppermute(same, TIME, route(1, 0))
        own_cross = lax.ppermute(cross, TIME, route(0, 1))
    coef = jnp.broadcast_to(taps_coef[:, :, None], taps_coef.shape + (LANES,))
    high, low = fourier_table(samples)
    valid = lax.dynamic_slice_in_dim((1 - flags).astype(F32), core * LANES, LANES)[None, :]
    place = jnp.stack([core, (chip == chips - 1).astype(jnp.int32)]).astype(jnp.int32)
    dests, parts = chips * cores, 2
    with jax.named_scope("filter"):
        spectra = filter_bank(
            place,
            (same, own_cross, left_same, left_cross, right_same, right_cross),
            coef, high, low, valid, dests, parts,
        )

    inputs = width * rows
    order = jnp.arange(inputs, dtype=jnp.int32)
    held_input = (row + order // width) % rows * width + order % width
    pick = (held_input[:, None] == station_map[None, :]).astype(BF16)
    own_slots = lax.dynamic_slice_in_dim(station_map, row * width, width)
    pick_rows = (own_slots[:, None] == held_input[None, :]).astype(BF16)

    turned, gathered = [], []
    for spectrum in spectra:
        with jax.named_scope("exchange"):
            turned.append(lax.all_to_all(spectrum, TIME, 0, 0, tiled=True))
    shape = (samples // dests, 2, width, inputs)
    scale = 1.0 / (frames * dests)
    out = None
    per_part = shape[0] // parts
    for n, block in enumerate(turned):
        with jax.named_scope("gather"):
            blocks = [block] + [
                lax.ppermute(block, "inp", [((i + d) % rows, i) for i in range(rows)]) for d in range(1, rows)
            ]
        blocks = [b.reshape(chips, cores, -1, LANES) for b in blocks]
        with jax.named_scope("correlate"):
            out = correlate(blocks, pick, pick_rows, scale, 4 * frames, shape, n * per_part, out)
    return out


def solution(mesh):
    return jax.shard_map(
        local,
        mesh=mesh,
        in_specs=(P(("tm", "integ"), None, None, "inp"), P(), P(), P("inp")),
        out_specs=P(("tm", "integ"), None, "inp", None),
        check_vma=False,
    )
```

```python
import functools
import math

import jax
import jax.numpy as jnp
import ml_dtypes
import numpy as np
from jax import lax
from jax.experimental import pallas as pl
from jax.experimental.pallas import tpu as pltpu
from jax.sharding import PartitionSpec as P

TIME = ("tm", "integ")
BF16, F32 = jnp.bfloat16, jnp.float32
LANES = 128
HALF = LANES // 2
BATCHES = 2
VMEM = pl.BlockSpec(memory_space=pltpu.VMEM)
ANY = pl.BlockSpec(memory_space=pl.ANY)
SMEM = pl.BlockSpec(memory_space=pltpu.SMEM)


def fourier_table(channels):
    grid = np.arange(channels)
    angles = (grid[:, None] * grid[None, :] % channels) * (2.0 * math.pi / channels)
    table = np.concatenate([np.cos(angles), np.sin(angles)]) / math.sqrt(channels)
    high = table.astype(ml_dtypes.bfloat16)
    low = (table - high.astype(np.float64)).astype(ml_dtypes.bfloat16)
    return jnp.asarray(high), jnp.asarray(low)


def pack_kernel(voltages, same, cross):
    first = lax.broadcasted_iota(jnp.int32, (voltages.shape[2], LANES), 1) < HALF
    me = lax.axis_index("integ")

    def one_frame(frame, carry):
        for core, out in ((me, same), (1 - me, cross)):
            lanes = pl.ds(pl.multiple_of(core * LANES, LANES), LANES)
            real = voltages[frame, 0, :, lanes].astype(F32)
            imag = voltages[frame, 1, :, lanes].astype(F32)
            out[0, frame] = jnp.where(first, real, pltpu.roll(imag, HALF, 1)).astype(BF16)
            out[1, frame] = jnp.where(first, pltpu.roll(real, HALF, 1), imag).astype(BF16)
        return carry

    lax.fori_loop(0, voltages.shape[0], one_frame, 0)


def pack(voltages):
    frames, _, samples, _ = voltages.shape
    return pl.pallas_call(
        pack_kernel,
        out_shape=[jax.ShapeDtypeStruct((BATCHES, frames, samples, LANES), BF16)] * 2,
        in_specs=[VMEM],
        out_specs=[VMEM] * 2,
        name="pack",
    )(voltages)


def arrange_kernel(same, cross, *outs):
    frames = same.shape[1]
    me = lax.axis_index("integ")
    for batch, out in enumerate(outs):
        out[pl.ds(me * frames, frames)] = same[batch]
        out[pl.ds((1 - me) * frames, frames)] = cross[batch]


def arrange(same, cross):
    batches, frames, samples, _ = same.shape
    return pl.pallas_call(
        arrange_kernel,
        out_shape=[jax.ShapeDtypeStruct((2 * frames, samples, LANES), BF16)] * batches,
        in_specs=[VMEM] * 2,
        out_specs=[VMEM] * batches,
        name="arrange",
    )(same, cross)


def filter_kernel(
    taps, frames, place, left, own, right,
    coef, high, low, valid, out, held, w_high, w_low, turned, sems
):
    wraps = place[0]
    samples = own.shape[1]
    copies = []
    for n, block in enumerate((left, own, right)):
        copies.append(pltpu.make_async_copy(block, held.at[pl.ds(n * frames, frames)], sems.at[n]))
        copies[-1].start()
    for copy in copies:
        copy.wait()

    @pl.when(wraps >= 1)
    def _():
        held[:frames] = jnp.zeros((frames,) + own.shape[1:], BF16)

    @pl.when(wraps == 2)
    def _():
        held[frames : 2 * frames] = jnp.zeros((frames,) + own.shape[1:], BF16)

    rows = 16

    def one_block(block, carry):
        at = pl.ds(pl.multiple_of(block * rows, rows), rows)
        column = coef[at, :]
        factors = [jnp.broadcast_to(column[:, p : p + 1], (rows, LANES)) for p in range(taps)]
        sums = [None] * frames
        for j in range(2 * frames - taps + 1, 3 * frames):
            x = held[j, at, :].astype(F32)
            for o in range(frames):
                p = j - (2 * frames - taps + 1) - o
                if 0 <= p < taps:
                    term = factors[p] * x
                    sums[o] = term if sums[o] is None else sums[o] + term
        for o in range(frames):
            top = sums[o].astype(BF16)
            lanes = slice((o % 2) * LANES, (o % 2 + 1) * LANES)
            w_high[o // 2, at, lanes] = top
            w_low[o // 2, at, lanes] = (sums[o] - top.astype(F32)).astype(BF16)
        return carry

    lax.fori_loop(0, samples // rows, one_block, 0)

    keep = valid[...]
    sign = jnp.where(lax.broadcasted_iota(jnp.int32, (1, LANES), 1) < HALF, 1.0, -1.0).astype(F32)
    for pair in range(frames // 2):
        block = jnp.dot(high[...], w_high[pair], preferred_element_type=F32)
        block += jnp.dot(high[...], w_low[pair], preferred_element_type=F32)
        block += jnp.dot(low[...], w_high[pair], preferred_element_type=F32)
        for which in range(2):
            lanes = slice(which * LANES, (which + 1) * LANES)
            cosines, sines = block[:samples, lanes], block[samples:, lanes]
            spectrum = (cosines + sign * pltpu.roll(sines, HALF, 1)) * keep
            turned[pl.ds(pair * 2 + which, samples, stride=frames), :] = spectrum

    depth = out.shape[1]

    def one_dest(dest, carry):
        out[dest] = turned[pl.ds(pl.multiple_of(dest * depth, depth), depth), :].astype(BF16)
        return carry

    lax.fori_loop(0, out.shape[0], one_dest, 0, unroll=8)


def filter_bank(place, blocks, coef, high, low, valid, dests):
    samples, taps = coef.shape
    frames = blocks[0].shape[0]
    return pl.pallas_call(
        functools.partial(filter_kernel, taps, frames),
        out_shape=jax.ShapeDtypeStruct((dests, samples // dests * frames, LANES), BF16),
        in_specs=[SMEM] + [ANY] * 3 + [VMEM] * 4,
        out_specs=VMEM,
        scratch_shapes=[
            pltpu.VMEM((3 * frames, samples, LANES), BF16),
            pltpu.VMEM((frames // 2, samples, 2 * LANES), BF16),
            pltpu.VMEM((frames // 2, samples, 2 * LANES), BF16),
            pltpu.VMEM((samples * frames, LANES), F32),
            pltpu.SemaphoreType.DMA((3,)),
        ],
        compiler_params=pltpu.CompilerParams(vmem_limit_bytes=12 * 2**20),
        cost_estimate=pl.CostEstimate(flops=20000000000, bytes_accessed=2**20, transcendentals=0),
        name="filter_bank",
    )(place, *blocks, coef, high, low, valid)


def columns_of(pieces):
    first, second = (
        jnp.concatenate([p[:, core].reshape(-1, LANES) for p in pieces], axis=0).astype(F32) for core in range(2)
    )
    lower = lax.broadcasted_iota(jnp.int32, first.shape, 1) < HALF
    real = jnp.where(lower, first, pltpu.roll(second, HALF, 1))
    imag = jnp.where(lower, pltpu.roll(first, HALF, 1), second)
    return jnp.concatenate([real, imag], axis=0).astype(BF16)


def place_inputs(blocks, pick, pick_own, frames, channels):
    gathered = jnp.concatenate([columns_of(b) for b in blocks], axis=1)

    def split(table):
        product = jnp.dot(gathered, table[...], preferred_element_type=F32)
        product = product.reshape(2, -1, channels, frames, table.shape[1])
        return lambda part, channel: product[part, :, channel].reshape(-1, table.shape[1]).astype(BF16)

    every, own = split(pick), split(pick_own)
    result = []
    for channel in range(channels):
        columns = jnp.concatenate([every(0, channel), every(1, channel)], axis=0)
        real, imag = own(0, channel), own(1, channel)
        rows = jnp.concatenate(
            [jnp.concatenate([real, imag], axis=1), jnp.concatenate([imag, -real], axis=1)], axis=0
        )
        result.append((columns, rows))
    return result


def grouped(refs, counts):
    return [refs[sum(counts[:n]) :][:count] for n, count in enumerate(counts)]


def order_kernel(counts, frames, *refs):
    blocks, (pick, pick_own, every, own) = grouped(refs, counts), refs[sum(counts) :]
    for channel, (columns, rows) in enumerate(place_inputs(blocks, pick, pick_own, frames, every.shape[0])):
        every[channel] = columns
        own[channel] = rows


def order_inputs(blocks, picks, frames):
    counts = [len(b) for b in blocks]
    operands = [piece for b in blocks for piece in b] + [*picks]
    channels = blocks[0][0].shape[2] // frames
    depth = 2 * frames * sum(p.shape[0] for p in blocks[0])
    shapes = [(channels, depth, picks[0].shape[1]), (channels, depth, 2 * picks[1].shape[1])]
    flops = 2 * channels * depth * picks[0].shape[0] * (picks[0].shape[1] + picks[1].shape[1])
    return pl.pallas_call(
        functools.partial(order_kernel, counts, frames),
        out_shape=[jax.ShapeDtypeStruct(shape, BF16) for shape in shapes],
        in_specs=[VMEM] * len(operands),
        out_specs=[VMEM] * 2,
        compiler_params=pltpu.CompilerParams(vmem_limit_bytes=30 * 2**20),
        cost_estimate=pl.CostEstimate(flops=flops, bytes_accessed=2**20, transcendentals=0),
        name="order_inputs",
    )(*operands)


def correlate_kernel(scale, counts, frames, *refs):
    blocks, (pick, pick_own, early, early_own, out, every, own) = grouped(refs, counts), refs[sum(counts) :]
    channel = pl.program_id(0)
    width = out.shape[2]

    @pl.when(channel == 0)
    def _():
        for n, (columns, rows) in enumerate(place_inputs(blocks, pick, pick_own, frames, every.shape[0])):
            every[n] = columns + early[n]
            own[n] = rows + early_own[n]

    product = lax.dot_general(
        own[channel], every[channel], (((0,), (0,)), ((), ())), preferred_element_type=F32
    )
    out[0, 0] = product[:width] * scale
    out[0, 1] = product[width:] * scale


def correlate(blocks, picks, early, scale, frames, shape):
    counts = [len(b) for b in blocks]
    operands = [piece for b in blocks for piece in b] + [*picks, *early]
    return pl.pallas_call(
        functools.partial(correlate_kernel, scale, counts, frames),
        grid=(shape[0],),
        out_shape=jax.ShapeDtypeStruct(shape, F32),
        in_specs=[VMEM] * len(operands),
        out_specs=pl.BlockSpec((1,) + shape[1:], lambda i: (i, 0, 0, 0)),
        scratch_shapes=[pltpu.VMEM(a.shape, BF16) for a in early],
        compiler_params=pltpu.CompilerParams(vmem_limit_bytes=32 * 2**20),
        name="correlate",
    )(*operands)


def local(voltages, taps_coef, station_map, flags):
    frames, _, samples, width = voltages.shape
    chips, cores, rows = lax.axis_size("tm"), lax.axis_size("integ"), lax.axis_size("inp")
    chip, core, row = lax.axis_index("tm"), lax.axis_index("integ"), lax.axis_index("inp")
    index = lambda t, c: t * cores + c
    dests, chip_frames, inputs = chips * cores, frames * cores, width * rows
    wraps = jnp.where(chip == chips - 1, 2, jnp.where(chip == 0, 1, 0))
    place = wraps.astype(jnp.int32)[None]

    def route(step, swap):
        return [(index((t - step) % chips, c ^ swap), index(t, c)) for t in range(chips) for c in range(cores)]

    with jax.named_scope("halo"):
        same, cross = pack(voltages)
        owns = arrange(same, lax.ppermute(cross, TIME, route(0, 1)))
        halos = [(lax.ppermute(o, TIME, route(1, 0)), o, lax.ppermute(o, TIME, route(-1, 0))) for o in owns]

    coef = taps_coef.T
    high, low = fourier_table(samples)
    valid = (1 - flags).astype(F32)

    own_slots = lax.dynamic_slice_in_dim(station_map, row * width, width)

    def picks(blocks):
        at = jnp.arange(LANES, dtype=jnp.int32)
        held = [(row + turn) % rows * width + at // HALF * LANES + batch * HALF + at % HALF for turn, batch in blocks]
        held = jnp.concatenate(held)
        return [(held[:, None] == slots[None, :]).astype(BF16) for slots in (station_map, own_slots)]

    up = [((i + 1) % rows, i) for i in range(rows)]
    down = [((i - 1) % rows, i) for i in range(rows)]
    shape = (samples // dests, 2, width, inputs)
    scale = 1.0 / (frames * dests)
    near, far = [], []
    for batch in range(BATCHES):
        flagged = lax.dynamic_slice_in_dim(valid, core * LANES + batch * HALF, HALF)
        keep = jnp.concatenate([flagged, flagged])[None, :]
        with jax.named_scope("filter"):
            spectra = filter_bank(place, halos[batch], coef, high, low, keep, dests)
        with jax.named_scope("exchange"):
            block = lax.all_to_all(spectra, TIME, 0, 0, tiled=True)
        block = block.reshape(chips, cores, -1, LANES)
        with jax.named_scope("gather"):
            above, below = lax.ppermute(block, "inp", up), lax.ppermute(block, "inp", down)
            half = chips // 2
            far.append([lax.ppermute(above[:half], "inp", up), lax.ppermute(below[half:], "inp", down)])
        near += [[block], [above], [below]]
    with jax.named_scope("order"):
        table = picks([(turn, batch) for batch in range(BATCHES) for turn in (0, 1, 3)])
        early = order_inputs(near, table, chip_frames)
    with jax.named_scope("correlate"):
        out = correlate(far, picks([(2, batch) for batch in range(BATCHES)]), early, scale, chip_frames, shape)
    return out


def solution(mesh):
    return jax.shard_map(
        local,
        mesh=mesh,
        in_specs=(P(("tm", "integ"), None, None, "inp"), P(), P(), P("inp")),
        out_specs=P(("tm", "integ"), None, "inp", None),
        check_vma=False,
    )
```

```python
import functools
import math

import jax
import jax.numpy as jnp
import ml_dtypes
import numpy as np
from jax import lax
from jax.experimental import pallas as pl
from jax.experimental.pallas import tpu as pltpu
from jax.sharding import PartitionSpec as P

TIME = ("tm", "integ")
BF16, F32 = jnp.bfloat16, jnp.float32
LANES = 128
HALF = LANES // 2
BATCHES = 2
VMEM = pl.BlockSpec(memory_space=pltpu.VMEM)
ANY = pl.BlockSpec(memory_space=pl.ANY)
SMEM = pl.BlockSpec(memory_space=pltpu.SMEM)


def fourier_table(channels):
    grid = np.arange(channels)
    angles = (grid[:, None] * grid[None, :] % channels) * (2.0 * math.pi / channels)
    table = np.concatenate([np.cos(angles), np.sin(angles)]) / math.sqrt(channels)
    high = table.astype(ml_dtypes.bfloat16)
    low = (table - high.astype(np.float64)).astype(ml_dtypes.bfloat16)
    return jnp.asarray(np.stack([high, low]))


def stage_kernel(source, out):
    out[...] = source[...]


def stage(table):
    return pl.pallas_call(
        stage_kernel,
        out_shape=jax.ShapeDtypeStruct(table.shape, table.dtype),
        in_specs=[VMEM],
        out_specs=VMEM,
        compiler_params=pltpu.CompilerParams(vmem_limit_bytes=4 * 2**20),
        name="stage",
    )(table)


def pack_kernel(voltages, same, cross):
    first = lax.broadcasted_iota(jnp.int32, (voltages.shape[2], LANES), 1) < HALF
    me = lax.axis_index("integ")

    def one_frame(frame, carry):
        for core, out in ((me, same), (1 - me, cross)):
            lanes = pl.ds(pl.multiple_of(core * LANES, LANES), LANES)
            real = voltages[frame, 0, :, lanes].astype(F32)
            imag = voltages[frame, 1, :, lanes].astype(F32)
            out[0, frame] = jnp.where(first, real, pltpu.roll(imag, HALF, 1)).astype(BF16)
            out[1, frame] = jnp.where(first, pltpu.roll(real, HALF, 1), imag).astype(BF16)
        return carry

    lax.fori_loop(0, voltages.shape[0], one_frame, 0)


def pack(voltages):
    frames, _, samples, _ = voltages.shape
    return pl.pallas_call(
        pack_kernel,
        out_shape=[jax.ShapeDtypeStruct((BATCHES, frames, samples, LANES), BF16)] * 2,
        in_specs=[VMEM],
        out_specs=[VMEM] * 2,
        compiler_params=pltpu.CompilerParams(vmem_limit_bytes=4 * 2**20),
        name="pack",
    )(voltages)


def arrange_kernel(same, cross, *outs):
    frames = same.shape[1]
    me = lax.axis_index("integ")
    for batch, out in enumerate(outs):
        out[pl.ds(me * frames, frames)] = same[batch]
        out[pl.ds((1 - me) * frames, frames)] = cross[batch]


def arrange(same, cross):
    batches, frames, samples, _ = same.shape
    return pl.pallas_call(
        arrange_kernel,
        out_shape=[jax.ShapeDtypeStruct((2 * frames, samples, LANES), BF16)] * batches,
        in_specs=[VMEM] * 2,
        out_specs=[VMEM] * batches,
        compiler_params=pltpu.CompilerParams(vmem_limit_bytes=4 * 2**20),
        name="arrange",
    )(same, cross)


def filter_kernel(
    taps, frames, place, left, own, right,
    coef, table, valid, out, held, w_high, w_low, turned, sems
):
    wraps = place[0]
    samples = own.shape[1]
    copies = []
    for n, block in enumerate((left, own, right)):
        copies.append(pltpu.make_async_copy(block, held.at[pl.ds(n * frames, frames)], sems.at[n]))
        copies[-1].start()
    for copy in copies:
        copy.wait()

    @pl.when(wraps >= 1)
    def _():
        held[:frames] = jnp.zeros((frames,) + own.shape[1:], BF16)

    @pl.when(wraps == 2)
    def _():
        held[frames : 2 * frames] = jnp.zeros((frames,) + own.shape[1:], BF16)

    rows = 16

    def one_block(block, carry):
        at = pl.ds(pl.multiple_of(block * rows, rows), rows)
        column = coef[at, :]
        factors = [jnp.broadcast_to(column[:, p : p + 1], (rows, LANES)) for p in range(taps)]
        sums = [None] * frames
        for j in range(2 * frames - taps + 1, 3 * frames):
            x = held[j, at, :].astype(F32)
            for o in range(frames):
                p = j - (2 * frames - taps + 1) - o
                if 0 <= p < taps:
                    term = factors[p] * x
                    sums[o] = term if sums[o] is None else sums[o] + term
        for o in range(frames):
            top = sums[o].astype(BF16)
            lanes = slice((o % 2) * LANES, (o % 2 + 1) * LANES)
            w_high[o // 2, at, lanes] = top
            w_low[o // 2, at, lanes] = (sums[o] - top.astype(F32)).astype(BF16)
        return carry

    lax.fori_loop(0, samples // rows, one_block, 0)

    keep = valid[...]
    sign = jnp.where(lax.broadcasted_iota(jnp.int32, (1, LANES), 1) < HALF, 1.0, -1.0).astype(F32)
    for pair in range(frames // 2):
        block = jnp.dot(table[0], w_high[pair], preferred_element_type=F32)
        block += jnp.dot(table[0], w_low[pair], preferred_element_type=F32)
        block += jnp.dot(table[1], w_high[pair], preferred_element_type=F32)
        for which in range(2):
            lanes = slice(which * LANES, (which + 1) * LANES)
            cosines, sines = block[:samples, lanes], block[samples:, lanes]
            spectrum = (cosines + sign * pltpu.roll(sines, HALF, 1)) * keep
            turned[pl.ds(pair * 2 + which, samples, stride=frames), :] = spectrum

    depth = out.shape[1]

    def one_dest(dest, carry):
        out[dest] = turned[pl.ds(pl.multiple_of(dest * depth, depth), depth), :].astype(BF16)
        return carry

    lax.fori_loop(0, out.shape[0], one_dest, 0, unroll=8)


def filter_bank(place, blocks, coef, table, valid, dests):
    samples, taps = coef.shape
    frames = blocks[0].shape[0]
    return pl.pallas_call(
        functools.partial(filter_kernel, taps, frames),
        out_shape=jax.ShapeDtypeStruct((dests, samples // dests * frames, LANES), BF16),
        in_specs=[SMEM] + [ANY] * 3 + [VMEM] * 3,
        out_specs=VMEM,
        scratch_shapes=[
            pltpu.VMEM((3 * frames, samples, LANES), BF16),
            pltpu.VMEM((frames // 2, samples, 2 * LANES), BF16),
            pltpu.VMEM((frames // 2, samples, 2 * LANES), BF16),
            pltpu.VMEM((samples * frames, LANES), F32),
            pltpu.SemaphoreType.DMA((3,)),
        ],
        compiler_params=pltpu.CompilerParams(vmem_limit_bytes=12 * 2**20),
        cost_estimate=pl.CostEstimate(flops=20000000000, bytes_accessed=2**20, transcendentals=0),
        name="filter_bank",
    )(place, *blocks, coef, table, valid)


def columns_of(pieces):
    first, second = (
        jnp.concatenate([p[:, core].reshape(-1, LANES) for p in pieces], axis=0).astype(F32) for core in range(2)
    )
    lower = lax.broadcasted_iota(jnp.int32, first.shape, 1) < HALF
    real = jnp.where(lower, first, pltpu.roll(second, HALF, 1))
    imag = jnp.where(lower, pltpu.roll(first, HALF, 1), second)
    return jnp.concatenate([real, imag], axis=0).astype(BF16)


def place_inputs(blocks, pick, pick_own, frames, channels):
    gathered = jnp.concatenate([columns_of(b) for b in blocks], axis=1)

    def split(table):
        product = jnp.dot(gathered, table[...], preferred_element_type=F32)
        product = product.reshape(2, -1, channels, frames, table.shape[1])
        return lambda part, channel: product[part, :, channel].reshape(-1, table.shape[1]).astype(BF16)

    every, own = split(pick), split(pick_own)
    result = []
    for channel in range(channels):
        columns = jnp.concatenate([every(0, channel), every(1, channel)], axis=0)
        real, imag = own(0, channel), own(1, channel)
        rows = jnp.concatenate(
            [jnp.concatenate([real, imag], axis=1), jnp.concatenate([imag, -real], axis=1)], axis=0
        )
        result.append((columns, rows))
    return result


def grouped(refs, counts):
    return [refs[sum(counts[:n]) :][:count] for n, count in enumerate(counts)]


def order_kernel(counts, frames, *refs):
    blocks, (pick, pick_own, every, own) = grouped(refs, counts), refs[sum(counts) :]
    for channel, (columns, rows) in enumerate(place_inputs(blocks, pick, pick_own, frames, every.shape[0])):
        every[channel] = columns
        own[channel] = rows


def order_inputs(blocks, picks, frames):
    counts = [len(b) for b in blocks]
    operands = [piece for b in blocks for piece in b] + [*picks]
    channels = blocks[0][0].shape[2] // frames
    depth = 2 * frames * sum(p.shape[0] for p in blocks[0])
    shapes = [(channels, depth, picks[0].shape[1]), (channels, depth, 2 * picks[1].shape[1])]
    flops = 2 * channels * depth * picks[0].shape[0] * (picks[0].shape[1] + picks[1].shape[1])
    return pl.pallas_call(
        functools.partial(order_kernel, counts, frames),
        out_shape=[jax.ShapeDtypeStruct(shape, BF16) for shape in shapes],
        in_specs=[VMEM] * len(operands),
        out_specs=[VMEM] * 2,
        compiler_params=pltpu.CompilerParams(vmem_limit_bytes=30 * 2**20),
        cost_estimate=pl.CostEstimate(flops=flops, bytes_accessed=2**20, transcendentals=0),
        name="order_inputs",
    )(*operands)


def correlate_kernel(scale, counts, frames, *refs):
    blocks, (pick, pick_own, early, early_own, out, every, own) = grouped(refs, counts), refs[sum(counts) :]
    channel = pl.program_id(0)
    width = out.shape[2]

    @pl.when(channel == 0)
    def _():
        for n, (columns, rows) in enumerate(place_inputs(blocks, pick, pick_own, frames, every.shape[0])):
            every[n] = columns + early[n]
            own[n] = rows + early_own[n]

    product = lax.dot_general(
        own[channel], every[channel], (((0,), (0,)), ((), ())), preferred_element_type=F32
    )
    out[0, 0] = product[:width] * scale
    out[0, 1] = product[width:] * scale


def correlate(blocks, picks, early, scale, frames, shape):
    counts = [len(b) for b in blocks]
    operands = [piece for b in blocks for piece in b] + [*picks, *early]
    return pl.pallas_call(
        functools.partial(correlate_kernel, scale, counts, frames),
        grid=(shape[0],),
        out_shape=jax.ShapeDtypeStruct(shape, F32),
        in_specs=[VMEM] * len(operands),
        out_specs=pl.BlockSpec((1,) + shape[1:], lambda i: (i, 0, 0, 0)),
        scratch_shapes=[pltpu.VMEM(a.shape, BF16) for a in early],
        compiler_params=pltpu.CompilerParams(vmem_limit_bytes=32 * 2**20),
        name="correlate",
    )(*operands)


def local(voltages, taps_coef, station_map, flags):
    frames, _, samples, width = voltages.shape
    chips, cores, rows = lax.axis_size("tm"), lax.axis_size("integ"), lax.axis_size("inp")
    chip, core, row = lax.axis_index("tm"), lax.axis_index("integ"), lax.axis_index("inp")
    index = lambda t, c: t * cores + c
    dests, chip_frames, inputs = chips * cores, frames * cores, width * rows
    wraps = jnp.where(chip == chips - 1, 2, jnp.where(chip == 0, 1, 0))
    place = wraps.astype(jnp.int32)[None]

    def route(step, swap):
        return [(index((t - step) % chips, c ^ swap), index(t, c)) for t in range(chips) for c in range(cores)]

    with jax.named_scope("halo"):
        same, cross = pack(voltages)
        owns = arrange(same, lax.ppermute(cross, TIME, route(0, 1)))
        halos = [(lax.ppermute(o, TIME, route(1, 0)), o, lax.ppermute(o, TIME, route(-1, 0))) for o in owns]

    coef = taps_coef.T
    table = stage(fourier_table(samples))
    valid = (1 - flags).astype(F32)

    own_slots = lax.dynamic_slice_in_dim(station_map, row * width, width)

    def picks(blocks):
        at = jnp.arange(LANES, dtype=jnp.int32)
        held = [(row + turn) % rows * width + at // HALF * LANES + batch * HALF + at % HALF for turn, batch in blocks]
        held = jnp.concatenate(held)
        return [(held[:, None] == slots[None, :]).astype(BF16) for slots in (station_map, own_slots)]

    up = [((i + 1) % rows, i) for i in range(rows)]
    down = [((i - 1) % rows, i) for i in range(rows)]
    shape = (samples // dests, 2, width, inputs)
    scale = 1.0 / (frames * dests)
    near, far = [], []
    for batch in range(BATCHES):
        flagged = lax.dynamic_slice_in_dim(valid, core * LANES + batch * HALF, HALF)
        keep = jnp.concatenate([flagged, flagged])[None, :]
        with jax.named_scope("filter"):
            spectra = filter_bank(place, halos[batch], coef, table, keep, dests)
        with jax.named_scope("exchange"):
            block = lax.all_to_all(spectra, TIME, 0, 0, tiled=True)
        block = block.reshape(chips, cores, -1, LANES)
        with jax.named_scope("gather"):
            above, below = lax.ppermute(block, "inp", up), lax.ppermute(block, "inp", down)
            half = chips // 2
            far.append([lax.ppermute(above[:half], "inp", up), lax.ppermute(below[half:], "inp", down)])
        near += [[block], [above], [below]]
    with jax.named_scope("order"):
        tables = picks([(turn, batch) for batch in range(BATCHES) for turn in (0, 1, 3)])
        early = order_inputs(near, tables, chip_frames)
    with jax.named_scope("correlate"):
        out = correlate(far, picks([(2, batch) for batch in range(BATCHES)]), early, scale, chip_frames, shape)
    return out


def solution(mesh):
    return jax.shard_map(
        local,
        mesh=mesh,
        in_specs=(P(("tm", "integ"), None, None, "inp"), P(), P(), P("inp")),
        out_specs=P(("tm", "integ"), None, "inp", None),
        check_vma=False,
    )
```

```python
import functools
import math

import jax
import jax.numpy as jnp
import ml_dtypes
import numpy as np
from jax import lax
from jax.experimental import pallas as pl
from jax.experimental.pallas import tpu as pltpu
from jax.sharding import PartitionSpec as P

TIME = ("tm", "integ")
BF16, F32 = jnp.bfloat16, jnp.float32
LANES = 128
HALF = LANES // 2
BATCHES = 2
VMEM = pl.BlockSpec(memory_space=pltpu.VMEM)
ANY = pl.BlockSpec(memory_space=pl.ANY)
SMEM = pl.BlockSpec(memory_space=pltpu.SMEM)


def fourier_table(channels):
    grid = np.arange(channels)
    angles = (grid[:, None] * grid[None, :] % channels) * (2.0 * math.pi / channels)
    table = np.concatenate([np.cos(angles), np.sin(angles)]) / math.sqrt(channels)
    high = table.astype(ml_dtypes.bfloat16)
    low = (table - high.astype(np.float64)).astype(ml_dtypes.bfloat16)
    return jnp.asarray(np.stack([high, low]))


def stage_kernel(source, out):
    out[...] = source[...]


def stage(table):
    return pl.pallas_call(
        stage_kernel,
        out_shape=jax.ShapeDtypeStruct(table.shape, table.dtype),
        in_specs=[VMEM],
        out_specs=VMEM,
        compiler_params=pltpu.CompilerParams(vmem_limit_bytes=4 * 2**20),
        name="stage",
    )(table)


def pack_kernel(voltages, same, cross):
    first = lax.broadcasted_iota(jnp.int32, (voltages.shape[2], LANES), 1) < HALF
    me = lax.axis_index("integ")

    def one_frame(frame, carry):
        for core, out in ((me, same), (1 - me, cross)):
            lanes = pl.ds(pl.multiple_of(core * LANES, LANES), LANES)
            real = voltages[frame, 0, :, lanes].astype(F32)
            imag = voltages[frame, 1, :, lanes].astype(F32)
            out[0, frame] = jnp.where(first, real, pltpu.roll(imag, HALF, 1)).astype(BF16)
            out[1, frame] = jnp.where(first, pltpu.roll(real, HALF, 1), imag).astype(BF16)
        return carry

    lax.fori_loop(0, voltages.shape[0], one_frame, 0)


def pack(voltages):
    frames, _, samples, _ = voltages.shape
    return pl.pallas_call(
        pack_kernel,
        out_shape=[jax.ShapeDtypeStruct((BATCHES, frames, samples, LANES), BF16)] * 2,
        in_specs=[VMEM],
        out_specs=[VMEM] * 2,
        compiler_params=pltpu.CompilerParams(vmem_limit_bytes=4 * 2**20),
        name="pack",
    )(voltages)


def arrange_kernel(same, cross, *outs):
    frames = same.shape[1]
    me = lax.axis_index("integ")
    for batch, out in enumerate(outs):
        out[pl.ds(me * frames, frames)] = same[batch]
        out[pl.ds((1 - me) * frames, frames)] = cross[batch]


def arrange(same, cross):
    batches, frames, samples, _ = same.shape
    return pl.pallas_call(
        arrange_kernel,
        out_shape=[jax.ShapeDtypeStruct((2 * frames, samples, LANES), BF16)] * batches,
        in_specs=[VMEM] * 2,
        out_specs=[VMEM] * batches,
        compiler_params=pltpu.CompilerParams(vmem_limit_bytes=4 * 2**20),
        name="arrange",
    )(same, cross)


def filter_kernel(
    taps, frames, place, left, own, right,
    coef, table, valid, out, held, w_high, w_low, turned, sems
):
    wraps = place[0]
    samples = own.shape[1]
    copies = []
    for n, block in enumerate((left, own, right)):
        copies.append(pltpu.make_async_copy(block, held.at[pl.ds(n * frames, frames)], sems.at[n]))
        copies[-1].start()
    for copy in copies:
        copy.wait()

    @pl.when(wraps >= 1)
    def _():
        held[:frames] = jnp.zeros((frames,) + own.shape[1:], BF16)

    @pl.when(wraps == 2)
    def _():
        held[frames : 2 * frames] = jnp.zeros((frames,) + own.shape[1:], BF16)

    rows = 16

    def one_block(block, carry):
        at = pl.ds(pl.multiple_of(block * rows, rows), rows)
        column = coef[at, :]
        factors = [jnp.broadcast_to(column[:, p : p + 1], (rows, LANES)) for p in range(taps)]
        sums = [None] * frames
        for j in range(2 * frames - taps + 1, 3 * frames):
            x = held[j, at, :].astype(F32)
            for o in range(frames):
                p = j - (2 * frames - taps + 1) - o
                if 0 <= p < taps:
                    term = factors[p] * x
                    sums[o] = term if sums[o] is None else sums[o] + term
        for o in range(frames):
            top = sums[o].astype(BF16)
            lanes = slice((o % 2) * LANES, (o % 2 + 1) * LANES)
            w_high[o // 2, at, lanes] = top
            w_low[o // 2, at, lanes] = (sums[o] - top.astype(F32)).astype(BF16)
        return carry

    lax.fori_loop(0, samples // rows, one_block, 0)

    keep = valid[...]
    sign = jnp.where(lax.broadcasted_iota(jnp.int32, (1, LANES), 1) < HALF, 1.0, -1.0).astype(F32)
    for pair in range(frames // 2):
        block = jnp.dot(table[0], w_high[pair], preferred_element_type=F32)
        block += jnp.dot(table[0], w_low[pair], preferred_element_type=F32)
        block += jnp.dot(table[1], w_high[pair], preferred_element_type=F32)
        for which in range(2):
            lanes = slice(which * LANES, (which + 1) * LANES)
            cosines, sines = block[:samples, lanes], block[samples:, lanes]
            spectrum = (cosines + sign * pltpu.roll(sines, HALF, 1)) * keep
            turned[pl.ds(pair * 2 + which, samples, stride=frames), :] = spectrum

    depth = out.shape[1]

    def one_dest(dest, carry):
        out[dest] = turned[pl.ds(pl.multiple_of(dest * depth, depth), depth), :].astype(BF16)
        return carry

    lax.fori_loop(0, out.shape[0], one_dest, 0, unroll=8)


def filter_bank(place, blocks, coef, table, valid, dests):
    samples, taps = coef.shape
    frames = blocks[0].shape[0]
    return pl.pallas_call(
        functools.partial(filter_kernel, taps, frames),
        out_shape=jax.ShapeDtypeStruct((dests, samples // dests * frames, LANES), BF16),
        in_specs=[SMEM] + [ANY] * 3 + [VMEM] * 3,
        out_specs=VMEM,
        scratch_shapes=[
            pltpu.VMEM((3 * frames, samples, LANES), BF16),
            pltpu.VMEM((frames // 2, samples, 2 * LANES), BF16),
            pltpu.VMEM((frames // 2, samples, 2 * LANES), BF16),
            pltpu.VMEM((samples * frames, LANES), F32),
            pltpu.SemaphoreType.DMA((3,)),
        ],
        compiler_params=pltpu.CompilerParams(vmem_limit_bytes=12 * 2**20),
        cost_estimate=pl.CostEstimate(flops=20000000000, bytes_accessed=2**20, transcendentals=0),
        name="filter_bank",
    )(place, *blocks, coef, table, valid)


def columns_of(pieces):
    first, second = (
        jnp.concatenate([p[:, core].reshape(-1, LANES) for p in pieces], axis=0).astype(F32) for core in range(2)
    )
    lower = lax.broadcasted_iota(jnp.int32, first.shape, 1) < HALF
    real = jnp.where(lower, first, pltpu.roll(second, HALF, 1))
    imag = jnp.where(lower, pltpu.roll(first, HALF, 1), second)
    return jnp.concatenate([real, imag], axis=0).astype(BF16)


def place_inputs(blocks, pick, pick_own, frames, channels):
    gathered = jnp.concatenate([columns_of(b) for b in blocks], axis=1)

    def split(table):
        product = jnp.dot(gathered, table[...], preferred_element_type=F32)
        product = product.reshape(2, -1, channels, frames, table.shape[1])
        return lambda part, channel: product[part, :, channel].reshape(-1, table.shape[1]).astype(BF16)

    every, own = split(pick), split(pick_own)
    result = []
    for channel in range(channels):
        columns = jnp.concatenate([every(0, channel), every(1, channel)], axis=0)
        real, imag = own(0, channel), own(1, channel)
        rows = jnp.concatenate(
            [jnp.concatenate([real, imag], axis=1), jnp.concatenate([imag, -real], axis=1)], axis=0
        )
        result.append((columns, rows))
    return result


def grouped(refs, counts):
    blocks = []
    for n, count in enumerate(counts):
        group = refs[sum(counts[:n]) :][:count]
        if len(group[0].shape) > 4:
            blocks += [[group[0].at[row]] for row in range(group[0].shape[0])]
        else:
            blocks.append(group)
    return blocks


def order_kernel(counts, frames, *refs):
    blocks, (pick, pick_own, every, own) = grouped(refs, counts), refs[sum(counts) :]
    for channel, (columns, rows) in enumerate(place_inputs(blocks, pick, pick_own, frames, every.shape[0])):
        every[channel] = columns
        own[channel] = rows


def order_inputs(blocks, picks, frames):
    counts = [len(b) for b in blocks]
    operands = [piece for b in blocks for piece in b] + [*picks]
    channels = blocks[-1][0].shape[2] // frames
    depth = 2 * frames * sum(p.shape[0] for p in blocks[-1])
    shapes = [(channels, depth, picks[0].shape[1]), (channels, depth, 2 * picks[1].shape[1])]
    flops = 2 * channels * depth * picks[0].shape[0] * (picks[0].shape[1] + picks[1].shape[1])
    return pl.pallas_call(
        functools.partial(order_kernel, counts, frames),
        out_shape=[jax.ShapeDtypeStruct(shape, BF16) for shape in shapes],
        in_specs=[VMEM] * len(operands),
        out_specs=[VMEM] * 2,
        compiler_params=pltpu.CompilerParams(vmem_limit_bytes=30 * 2**20),
        cost_estimate=pl.CostEstimate(flops=flops, bytes_accessed=2**20, transcendentals=0),
        name="order_inputs",
    )(*operands)


def correlate_kernel(scale, counts, frames, *refs):
    blocks, (pick, pick_own, early, early_own, out, every, own) = grouped(refs, counts), refs[sum(counts) :]
    channel = pl.program_id(0)
    width = out.shape[2]

    @pl.when(channel == 0)
    def _():
        for n, (columns, rows) in enumerate(place_inputs(blocks, pick, pick_own, frames, every.shape[0])):
            every[n] = columns + early[n]
            own[n] = rows + early_own[n]

    product = lax.dot_general(
        own[channel], every[channel], (((0,), (0,)), ((), ())), preferred_element_type=F32
    )
    out[0, 0] = product[:width] * scale
    out[0, 1] = product[width:] * scale


def correlate(blocks, picks, early, scale, frames, shape):
    counts = [len(b) for b in blocks]
    operands = [piece for b in blocks for piece in b] + [*picks, *early]
    return pl.pallas_call(
        functools.partial(correlate_kernel, scale, counts, frames),
        grid=(shape[0],),
        out_shape=jax.ShapeDtypeStruct(shape, F32),
        in_specs=[VMEM] * len(operands),
        out_specs=pl.BlockSpec((1,) + shape[1:], lambda i: (i, 0, 0, 0)),
        scratch_shapes=[pltpu.VMEM(a.shape, BF16) for a in early],
        compiler_params=pltpu.CompilerParams(vmem_limit_bytes=32 * 2**20),
        name="correlate",
    )(*operands)


def local(voltages, taps_coef, station_map, flags):
    frames, _, samples, width = voltages.shape
    chips, cores, rows = lax.axis_size("tm"), lax.axis_size("integ"), lax.axis_size("inp")
    chip, core, row = lax.axis_index("tm"), lax.axis_index("integ"), lax.axis_index("inp")
    index = lambda t, c: t * cores + c
    dests, chip_frames, inputs = chips * cores, frames * cores, width * rows
    wraps = jnp.where(chip == chips - 1, 2, jnp.where(chip == 0, 1, 0))
    place = wraps.astype(jnp.int32)[None]

    def route(step, swap):
        return [(index((t - step) % chips, c ^ swap), index(t, c)) for t in range(chips) for c in range(cores)]

    with jax.named_scope("halo"):
        same, cross = pack(voltages)
        owns = arrange(same, lax.ppermute(cross, TIME, route(0, 1)))
        halos = [(lax.ppermute(o, TIME, route(1, 0)), o, lax.ppermute(o, TIME, route(-1, 0))) for o in owns]

    coef = taps_coef.T
    table = stage(fourier_table(samples))
    valid = (1 - flags).astype(F32)

    own_slots = lax.dynamic_slice_in_dim(station_map, row * width, width)

    def picks(blocks):
        at = jnp.arange(LANES, dtype=jnp.int32)
        held = [source * width + at // HALF * LANES + batch * HALF + at % HALF for source, batch in blocks]
        held = jnp.concatenate(held)
        return [(held[:, None] == slots[None, :]).astype(BF16) for slots in (station_map, own_slots)]

    up = [((i + 1) % rows, i) for i in range(rows)]
    down = [((i - 1) % rows, i) for i in range(rows)]
    shape = (samples // dests, 2, width, inputs)
    scale = 1.0 / (frames * dests)
    near, sources = [], []
    spectra = []
    for batch in range(BATCHES):
        flagged = lax.dynamic_slice_in_dim(valid, core * LANES + batch * HALF, HALF)
        keep = jnp.concatenate([flagged, flagged])[None, :]
        with jax.named_scope("filter"):
            spectrum = filter_bank(place, halos[batch], coef, table, keep, dests)
        spectra.append(spectrum)
    for batch in range(BATCHES):
        with jax.named_scope("exchange"):
            block = lax.all_to_all(spectra[batch], TIME, 0, 0, tiled=True)
            if batch < BATCHES - 1:
                block, spectra[batch + 1] = lax.optimization_barrier((block, spectra[batch + 1]))
        block = block.reshape(chips, cores, -1, LANES)
        with jax.named_scope("gather"):
            if batch < BATCHES - 1:
                near.append([lax.all_gather(block, "inp", axis=0)])
                sources += [(source, batch) for source in range(rows)]
                continue
            above, below = lax.ppermute(block, "inp", up), lax.ppermute(block, "inp", down)
            half = chips // 2
            far = [lax.ppermute(above[:half], "inp", up), lax.ppermute(below[half:], "inp", down)]
            near += [[block], [above], [below]]
            sources += [((row + turn) % rows, batch) for turn in (0, 1, 3)]
    with jax.named_scope("order"):
        early = order_inputs(near, picks(sources), chip_frames)
    with jax.named_scope("correlate"):
        out = correlate([far], picks([((row + 2) % rows, BATCHES - 1)]), early, scale, chip_frames, shape)
    return out


def solution(mesh):
    return jax.shard_map(
        local,
        mesh=mesh,
        in_specs=(P(("tm", "integ"), None, None, "inp"), P(), P(), P("inp")),
        out_specs=P(("tm", "integ"), None, "inp", None),
        check_vma=False,
    )
```

```python
import functools
import math

import jax
import jax.numpy as jnp
import ml_dtypes
import numpy as np
from jax import lax
from jax.experimental import pallas as pl
from jax.experimental.pallas import tpu as pltpu
from jax.sharding import PartitionSpec as P

TIME = ("tm", "integ")
BF16, F32 = jnp.bfloat16, jnp.float32
LANES = 128
HALF = LANES // 2
BATCHES = 2
VMEM = pl.BlockSpec(memory_space=pltpu.VMEM)
ANY = pl.BlockSpec(memory_space=pl.ANY)
SMEM = pl.BlockSpec(memory_space=pltpu.SMEM)


def fourier_table(channels):
    grid = np.arange(channels)
    angles = (grid[:, None] * grid[None, :] % channels) * (2.0 * math.pi / channels)
    table = np.concatenate([np.cos(angles), np.sin(angles)]) / math.sqrt(channels)
    high = table.astype(ml_dtypes.bfloat16)
    low = (table - high.astype(np.float64)).astype(ml_dtypes.bfloat16)
    return jnp.asarray(np.stack([high, low]))


def stage_kernel(source, out):
    out[...] = source[...]


def stage(table):
    return pl.pallas_call(
        stage_kernel,
        out_shape=jax.ShapeDtypeStruct(table.shape, table.dtype),
        in_specs=[VMEM],
        out_specs=VMEM,
        compiler_params=pltpu.CompilerParams(vmem_limit_bytes=4 * 2**20),
        name="stage",
    )(table)


def pack_kernel(voltages, same, cross):
    first = lax.broadcasted_iota(jnp.int32, (voltages.shape[2], LANES), 1) < HALF
    me = lax.axis_index("integ")

    def one_frame(frame, carry):
        for core, out in ((me, same), (1 - me, cross)):
            lanes = pl.ds(pl.multiple_of(core * LANES, LANES), LANES)
            real = voltages[frame, 0, :, lanes].astype(F32)
            imag = voltages[frame, 1, :, lanes].astype(F32)
            out[0, frame] = jnp.where(first, real, pltpu.roll(imag, HALF, 1)).astype(BF16)
            out[1, frame] = jnp.where(first, pltpu.roll(real, HALF, 1), imag).astype(BF16)
        return carry

    lax.fori_loop(0, voltages.shape[0], one_frame, 0)


def pack(voltages):
    frames, _, samples, _ = voltages.shape
    return pl.pallas_call(
        pack_kernel,
        out_shape=[jax.ShapeDtypeStruct((BATCHES, frames, samples, LANES), BF16)] * 2,
        in_specs=[VMEM],
        out_specs=[VMEM] * 2,
        compiler_params=pltpu.CompilerParams(vmem_limit_bytes=4 * 2**20),
        name="pack",
    )(voltages)


def arrange_kernel(same, cross, *outs):
    frames = same.shape[1]
    me = lax.axis_index("integ")
    for batch, out in enumerate(outs):
        out[pl.ds(me * frames, frames)] = same[batch]
        out[pl.ds((1 - me) * frames, frames)] = cross[batch]


def arrange(same, cross):
    batches, frames, samples, _ = same.shape
    return pl.pallas_call(
        arrange_kernel,
        out_shape=[jax.ShapeDtypeStruct((2 * frames, samples, LANES), BF16)] * batches,
        in_specs=[VMEM] * 2,
        out_specs=[VMEM] * batches,
        compiler_params=pltpu.CompilerParams(vmem_limit_bytes=4 * 2**20),
        name="arrange",
    )(same, cross)


def filter_kernel(
    taps, frames, place, left, own, right,
    coef, table, valid, out, held, w_high, w_low, turned, sems
):
    wraps = place[0]
    samples = own.shape[1]
    copies = []
    for n, block in enumerate((left, own, right)):
        copies.append(pltpu.make_async_copy(block, held.at[pl.ds(n * frames, frames)], sems.at[n]))
        copies[-1].start()
    for copy in copies:
        copy.wait()

    @pl.when(wraps >= 1)
    def _():
        held[:frames] = jnp.zeros((frames,) + own.shape[1:], BF16)

    @pl.when(wraps == 2)
    def _():
        held[frames : 2 * frames] = jnp.zeros((frames,) + own.shape[1:], BF16)

    rows = 16

    def one_block(block, carry):
        at = pl.ds(pl.multiple_of(block * rows, rows), rows)
        column = coef[at, :]
        factors = [jnp.broadcast_to(column[:, p : p + 1], (rows, LANES)) for p in range(taps)]
        sums = [None] * frames
        for j in range(2 * frames - taps + 1, 3 * frames):
            x = held[j, at, :].astype(F32)
            for o in range(frames):
                p = j - (2 * frames - taps + 1) - o
                if 0 <= p < taps:
                    term = factors[p] * x
                    sums[o] = term if sums[o] is None else sums[o] + term
        for o in range(frames):
            top = sums[o].astype(BF16)
            lanes = slice((o % 2) * LANES, (o % 2 + 1) * LANES)
            w_high[o // 2, at, lanes] = top
            w_low[o // 2, at, lanes] = (sums[o] - top.astype(F32)).astype(BF16)
        return carry

    lax.fori_loop(0, samples // rows, one_block, 0)

    keep = valid[...]
    sign = jnp.where(lax.broadcasted_iota(jnp.int32, (1, LANES), 1) < HALF, 1.0, -1.0).astype(F32)
    for pair in range(frames // 2):
        block = jnp.dot(table[0], w_high[pair], preferred_element_type=F32)
        block += jnp.dot(table[0], w_low[pair], preferred_element_type=F32)
        block += jnp.dot(table[1], w_high[pair], preferred_element_type=F32)
        for which in range(2):
            lanes = slice(which * LANES, (which + 1) * LANES)
            cosines, sines = block[:samples, lanes], block[samples:, lanes]
            spectrum = (cosines + sign * pltpu.roll(sines, HALF, 1)) * keep
            turned[pl.ds(pair * 2 + which, samples, stride=frames), :] = spectrum

    depth = out.shape[1]

    def one_dest(dest, carry):
        out[dest] = turned[pl.ds(pl.multiple_of(dest * depth, depth), depth), :].astype(BF16)
        return carry

    lax.fori_loop(0, out.shape[0], one_dest, 0, unroll=8)


def filter_bank(place, blocks, coef, table, valid, dests):
    samples, taps = coef.shape
    frames = blocks[0].shape[0]
    return pl.pallas_call(
        functools.partial(filter_kernel, taps, frames),
        out_shape=jax.ShapeDtypeStruct((dests, samples // dests * frames, LANES), BF16),
        in_specs=[SMEM] + [ANY] * 3 + [VMEM] * 3,
        out_specs=VMEM,
        scratch_shapes=[
            pltpu.VMEM((3 * frames, samples, LANES), BF16),
            pltpu.VMEM((frames // 2, samples, 2 * LANES), BF16),
            pltpu.VMEM((frames // 2, samples, 2 * LANES), BF16),
            pltpu.VMEM((samples * frames, LANES), F32),
            pltpu.SemaphoreType.DMA((3,)),
        ],
        compiler_params=pltpu.CompilerParams(vmem_limit_bytes=12 * 2**20),
        cost_estimate=pl.CostEstimate(flops=20000000000, bytes_accessed=2**20, transcendentals=0),
        name="filter_bank",
    )(place, *blocks, coef, table, valid)


def columns_of(pieces):
    first, second = (
        jnp.concatenate([p[:, core].reshape(-1, LANES) for p in pieces], axis=0).astype(F32) for core in range(2)
    )
    lower = lax.broadcasted_iota(jnp.int32, first.shape, 1) < HALF
    real = jnp.where(lower, first, pltpu.roll(second, HALF, 1))
    imag = jnp.where(lower, pltpu.roll(first, HALF, 1), second)
    return jnp.concatenate([real, imag], axis=0).astype(BF16)


def place_inputs(blocks, pick, pick_own, frames, channels):
    gathered = jnp.concatenate([columns_of(b) for b in blocks], axis=1)

    def split(table):
        product = jnp.dot(gathered, table[...], preferred_element_type=F32)
        product = product.reshape(2, -1, channels, frames, table.shape[1])
        return lambda part, channel: product[part, :, channel].reshape(-1, table.shape[1]).astype(BF16)

    every, own = split(pick), split(pick_own)
    result = []
    for channel in range(channels):
        columns = jnp.concatenate([every(0, channel), every(1, channel)], axis=0)
        real, imag = own(0, channel), own(1, channel)
        rows = jnp.concatenate(
            [jnp.concatenate([real, imag], axis=1), jnp.concatenate([imag, -real], axis=1)], axis=0
        )
        result.append((columns, rows))
    return result


def grouped(refs, counts):
    return [refs[sum(counts[:n]) :][:count] for n, count in enumerate(counts)]


def order_kernel(counts, frames, *refs):
    blocks, (pick, pick_own, every, own) = grouped(refs, counts), refs[sum(counts) :]
    for channel, (columns, rows) in enumerate(place_inputs(blocks, pick, pick_own, frames, every.shape[0])):
        every[channel] = columns
        own[channel] = rows


def order_inputs(blocks, picks, frames):
    counts = [len(b) for b in blocks]
    operands = [piece for b in blocks for piece in b] + [*picks]
    channels = blocks[0][0].shape[2] // frames
    depth = 2 * frames * sum(p.shape[0] for p in blocks[0])
    shapes = [(channels, depth, picks[0].shape[1]), (channels, depth, 2 * picks[1].shape[1])]
    flops = 2 * channels * depth * picks[0].shape[0] * (picks[0].shape[1] + picks[1].shape[1])
    return pl.pallas_call(
        functools.partial(order_kernel, counts, frames),
        out_shape=[jax.ShapeDtypeStruct(shape, BF16) for shape in shapes],
        in_specs=[VMEM] * len(operands),
        out_specs=[VMEM] * 2,
        compiler_params=pltpu.CompilerParams(vmem_limit_bytes=30 * 2**20),
        cost_estimate=pl.CostEstimate(flops=flops, bytes_accessed=2**20, transcendentals=0),
        name="order_inputs",
    )(*operands)


def correlate_kernel(scale, counts, frames, *refs):
    blocks, (pick, pick_own, early, early_own, out, every, own) = grouped(refs, counts), refs[sum(counts) :]
    channel = pl.program_id(0)
    width = out.shape[2]

    @pl.when(channel == 0)
    def _():
        for n, (columns, rows) in enumerate(place_inputs(blocks, pick, pick_own, frames, every.shape[0])):
            every[n] = columns + early[n]
            own[n] = rows + early_own[n]

    product = lax.dot_general(
        own[channel], every[channel], (((0,), (0,)), ((), ())), preferred_element_type=F32
    )
    out[0, 0] = product[:width] * scale
    out[0, 1] = product[width:] * scale


def correlate(blocks, picks, early, scale, frames, shape):
    counts = [len(b) for b in blocks]
    operands = [piece for b in blocks for piece in b] + [*picks, *early]
    return pl.pallas_call(
        functools.partial(correlate_kernel, scale, counts, frames),
        grid=(shape[0],),
        out_shape=jax.ShapeDtypeStruct(shape, F32),
        in_specs=[VMEM] * len(operands),
        out_specs=pl.BlockSpec((1,) + shape[1:], lambda i: (i, 0, 0, 0)),
        scratch_shapes=[pltpu.VMEM(a.shape, BF16) for a in early],
        compiler_params=pltpu.CompilerParams(vmem_limit_bytes=32 * 2**20),
        name="correlate",
    )(*operands)


def local(voltages, taps_coef, station_map, flags):
    frames, _, samples, width = voltages.shape
    chips, cores, rows = lax.axis_size("tm"), lax.axis_size("integ"), lax.axis_size("inp")
    chip, core, row = lax.axis_index("tm"), lax.axis_index("integ"), lax.axis_index("inp")
    index = lambda t, c: t * cores + c
    dests, chip_frames, inputs = chips * cores, frames * cores, width * rows
    wraps = jnp.where(chip == chips - 1, 2, jnp.where(chip == 0, 1, 0))
    place = wraps.astype(jnp.int32)[None]

    def route(step, swap):
        return [(index((t - step) % chips, c ^ swap), index(t, c)) for t in range(chips) for c in range(cores)]

    with jax.named_scope("halo"):
        same, cross = pack(voltages)
        owns = arrange(same, lax.ppermute(cross, TIME, route(0, 1)))
        halos = [(lax.ppermute(o, TIME, route(1, 0)), o, lax.ppermute(o, TIME, route(-1, 0))) for o in owns]

    coef = taps_coef.T
    table = stage(fourier_table(samples))
    valid = (1 - flags).astype(F32)

    own_slots = lax.dynamic_slice_in_dim(station_map, row * width, width)

    def picks(blocks):
        at = jnp.arange(LANES, dtype=jnp.int32)
        held = [(row + turn) % rows * width + at // HALF * LANES + batch * HALF + at % HALF for turn, batch in blocks]
        held = jnp.concatenate(held)
        return [(held[:, None] == slots[None, :]).astype(BF16) for slots in (station_map, own_slots)]

    up = [((i + 1) % rows, i) for i in range(rows)]
    down = [((i - 1) % rows, i) for i in range(rows)]
    shape = (samples // dests, 2, width, inputs)
    scale = 1.0 / (frames * dests)
    near, far = [], []
    for batch in range(BATCHES):
        flagged = lax.dynamic_slice_in_dim(valid, core * LANES + batch * HALF, HALF)
        keep = jnp.concatenate([flagged, flagged])[None, :]
        with jax.named_scope("filter"):
            spectra = filter_bank(place, halos[batch], coef, table, keep, dests)
        with jax.named_scope("exchange"):
            block = lax.all_to_all(spectra, TIME, 0, 0, tiled=True)
        block = block.reshape(chips, cores, -1, LANES)
        with jax.named_scope("gather"):
            above, below = lax.ppermute(block, "inp", up), lax.ppermute(block, "inp", down)
            half = chips // 2
            far.append([lax.ppermute(above[:half], "inp", up), lax.ppermute(below[half:], "inp", down)])
        near += [[block], [above], [below]]
    with jax.named_scope("order"):
        tables = picks([(turn, batch) for batch in range(BATCHES) for turn in (0, 1, 3)] + [(2, 0)])
        early = order_inputs(near + far[:1], tables, chip_frames)
    with jax.named_scope("correlate"):
        out = correlate(far[1:], picks([(2, batch) for batch in range(1, BATCHES)]), early, scale, chip_frames, shape)
    return out


def solution(mesh):
    return jax.shard_map(
        local,
        mesh=mesh,
        in_specs=(P(("tm", "integ"), None, None, "inp"), P(), P(), P("inp")),
        out_specs=P(("tm", "integ"), None, "inp", None),
        check_vma=False,
    )
```
